32 devices in a mesh: lat: 16 (over z, y, x), dp: 2 (over core).
Axes of the slice: x: 2, y: 2, z: 4, core: 2. Of those that a mesh axis runs over, the one named last changes fastest.
Arguments:
- inputs: bfloat16 [1024, 4096], P('dp', 'lat'), may hold values from -6 to 6
- dec_bias: bfloat16 [4096], P('lat'), may hold values from -3 to 3
- enc_weight: bfloat16 [4096, 4096], P(None, 'lat'), may hold values from -0.09375 to 0.09375
- enc_bias: float32 [4096], P('lat'), may hold values from -3 to 3
- dec_weight: bfloat16 [4096, 4096], P('lat'), may hold values from -0.09375 to 0.09375
- other_recon: float32 [1024, 4096], P('dp', 'lat'), may hold values from -6 to 6
- active_blocks: int32 [1024, 32], P('dp', 'lat'), may hold values 0 or 1
Outputs:
- error_full: float32 [1024, 4096], P('dp', 'lat')
- mse_loss: float32 [], replicated
- grad_dec: float32 [4096, 4096], P(('lat', 'dp'))
- grad_enc: float32 [4096, 4096], P(None, ('lat', 'dp'))
The draws below stay inside these ranges and needn't reach their ends.
All inputs are finite; a program needn't handle non-finite values. No bound on the sum of `active_blocks` on one device may be relied on, other than what follows from the above.
Results may differ from the reference program's by a relative error of at most 0.0033.
Values may be sent and summed in bfloat16 or wider, within the bound.
No kernel may reach another device: no remote copies, remote signals or barrier semaphores. Data moves between devices by JAX's collectives and lax.ppermute only.
A program may use at most 128 MiB of HBM per device.

```python
import jax
import jax.numpy as jnp
from jax import lax

D = 4096
BLOCK = 128
LATENTS = 4096
NBLK = 32
ROWS = 1024


def place_ends(drawn, stream_key, least, top_value):
    place = [jax.random.randint(jax.random.fold_in(stream_key, axis), (), 0, length) for axis, length in enumerate(drawn.shape)]
    longest = drawn.shape.index(max(drawn.shape))
    next_to = place[:longest] + [(place[longest] + 1) % drawn.shape[longest]] + place[longest + 1:]
    return drawn.at[tuple(place)].set(least).at[tuple(next_to)].set(top_value)


def block_levels(own_key, shape, pieces, least, top_value):
    def one(dim, blocks):
        draws = jax.random.uniform(jax.random.fold_in(jax.random.fold_in(own_key, 6), dim), (blocks,), jnp.float32, least / len(pieces), top_value / len(pieces))
        return jnp.repeat(jnp.exp(draws), shape[dim] // blocks).reshape((-1,) + (1,) * (len(shape) - dim - 1))

    loudness = one(*pieces[0])
    for cut in pieces[1:]:
        loudness = loudness * one(*cut)
    return loudness


def gaussian(stream_key, shape, width, most, cuts=(), dtype=jnp.bfloat16):
    values = jax.random.normal(stream_key, shape, jnp.float32) * width
    if len(cuts) > 0:
        values = block_levels(stream_key, shape, cuts, -0.22, 0.18) * values
    return jnp.clip(values, min=-most, max=most).astype(dtype)


def setup_inputs(seed: int = 0) -> dict:
    key_list = jax.random.split(jax.random.key(seed), 8)
    inputs = gaussian(key_list[0], (ROWS, D), 1.0, 6.0, ((0, 2), (1, 16)))
    dec_bias = gaussian(key_list[1], (D,), 0.5, 3.0, ((0, 16),))
    enc_weight = gaussian(key_list[2], (D, LATENTS), D ** -0.5, 0.09375, ((1, 16),))
    enc_bias = gaussian(key_list[3], (LATENTS,), 0.5, 3.0, ((0, 16),), jnp.float32)
    dec_weight = gaussian(key_list[4], (LATENTS, D), LATENTS ** -0.5, 0.09375, ((0, 16),))
    other_recon = gaussian(key_list[5], (ROWS, D), 1.0, 6.0, ((0, 2), (1, 16)), jnp.float32)
    active_blocks = place_ends((jax.random.randint(key_list[6], (ROWS, NBLK), 0, 3) < 1).astype(jnp.int32), jax.random.fold_in(key_list[6], 1), 0, 1)
    return {"inputs": inputs, "dec_bias": dec_bias, "enc_weight": enc_weight, "enc_bias": enc_bias, "dec_weight": dec_weight, "other_recon": other_recon, "active_blocks": active_blocks}


def reference(inputs, dec_bias, enc_weight, enc_bias, dec_weight, other_recon, active_blocks):
    centered = (inputs.astype(jnp.float32) - dec_bias.astype(jnp.float32)[None, :]).astype(jnp.bfloat16)
    pre_act = jnp.dot(centered, enc_weight, preferred_element_type=jnp.float32) + enc_bias[None, :]
    block_gate = jnp.repeat(active_blocks.astype(jnp.float32), BLOCK, axis=1)
    positive = jnp.maximum(pre_act, 0.0)
    activations = (positive * positive * block_gate).astype(jnp.bfloat16)
    recon = jnp.dot(activations, dec_weight, preferred_element_type=jnp.float32) + other_recon + dec_bias.astype(jnp.float32)[None, :]
    error_full = recon - inputs.astype(jnp.float32)
    mse_loss = jnp.mean(error_full * error_full)
    error_bf = error_full.astype(jnp.bfloat16)
    grad_dec = lax.dot_general(activations, error_bf, (((0,), (0,)), ((), ())), preferred_element_type=jnp.float32)
    dact = lax.dot_general(error_bf, dec_weight, (((1,), (1,)), ((), ())), preferred_element_type=jnp.float32)
    dpre = (dact * 2.0 * positive * block_gate).astype(jnp.bfloat16)
    grad_enc = lax.dot_general(centered, dpre, (((0,), (0,)), ((), ())), preferred_element_type=jnp.float32)
    return (error_full, mse_loss, grad_dec, grad_enc)
```

```python
import jax
import jax.numpy as jnp
from jax import lax
from jax.sharding import PartitionSpec as P


def _slot_table(planes):
    table = []
    for z in range(planes):
        near = [(d, s) for d in range(1, planes) for s in (1, -1) if 0 <= z + s * d < planes]
        table.append(near)
    return table


class Grid:
    def __init__(self, lat, dp):
        self.lat, self.dp, self.planes = lat, dp, lat // 4
        self.table = _slot_table(self.planes)
        self.me = lax.axis_index("lat")
        self.rank = lax.axis_index("dp")
        self.z = self.me // 4
        self.square = self.me % 4
        self.first = jnp.where(self.rank % 2 == 0, 1, 2)

    def send(self, x, pairs_of):
        pairs = []
        for i in range(self.lat):
            for d in range(self.dp):
                to = pairs_of(i, d)
                if to is not None:
                    pairs.append((i * self.dp + d, to * self.dp + d))
        return lax.ppermute(x, ("lat", "dp"), pairs)

    def swap_first(self, x):
        return self.send(x, lambda i, d: i ^ (1 if d % 2 == 0 else 2))

    def swap_second(self, x):
        return self.send(x, lambda i, d: i ^ (2 if d % 2 == 0 else 1))

    def shift(self, x, sign, sources):
        return self.send(x, lambda i, d: i + 4 * sign if i // 4 in sources else None)

    def pick(self, choices):
        kinds = []
        for c in choices:
            if c is not None and not any(c is k for k in kinds):
                kinds.append(c)
        out = kinds[0]
        for k in kinds[1:]:
            mine = [c is k for c in choices]
            out = jnp.where(jnp.array(mine)[self.z], k, out)
        return out

    def index(self, slot, member):
        if slot == 0:
            plane = self.z
        else:
            plane = jnp.array([z + s * d for z, (d, s) in enumerate(row[slot - 1] for row in self.table)])[self.z]
        change = (0, self.first, 3 - self.first, 3)[member]
        return 4 * plane + (self.square ^ change)

    def gather(self, own):
        planes = self.planes
        slots = [own]
        arrived = {}
        up, down = own, own
        for d in range(1, planes):
            up = self.shift(up, 1, range(d - 1, planes - 1))
            down = self.shift(down, -1, range(1, planes - d + 1))
            arrived[(d, -1)], arrived[(d, 1)] = up, down
        for k in range(planes - 1):
            slots.append(self.pick([arrived[self.table[z][k]] for z in range(planes)]))
        out = []
        for block in slots:
            a = self.swap_first(block)
            b = self.swap_second(block)
            c = self.swap_second(a)
            out.append((block, a, b, c))
        return out

    def scatter_sum(self, part):
        planes = self.planes
        column = [None] * planes
        for k in reversed(range(planes)):
            there = self.swap_second(
                jnp.stack([part(k, 2).astype(jnp.bfloat16), part(k, 3).astype(jnp.bfloat16)])
            )
            mine = part(k, 0) + there[0].astype(jnp.float32)
            other = part(k, 1) + there[1].astype(jnp.float32)
            column[k] = mine + self.swap_first(other.astype(jnp.bfloat16)).astype(jnp.float32)
        total = column[0]
        for sign in (1, -1):
            moving = None
            for d in reversed(range(1, planes)):
                sources = [z for z in range(planes) if 0 <= z + sign * d < planes]
                send = self.pick(
                    [column[1 + self.table[z].index((d, sign))] if z in sources else None for z in range(planes)]
                )
                if moving is not None:
                    send = send + moving
                moving = self.shift(send, sign, sources)
            total = total + moving
        return total

    def total(self, x):
        step = 1
        while step < self.dp:
            pairs = [(d, d ^ step) for d in range(self.dp)]
            x = x + lax.ppermute(x, "dp", pairs)
            step *= 2
        step = 1
        while step < self.lat:
            pairs = [(i, i ^ step) for i in range(self.lat)]
            x = x + lax.ppermute(x, "lat", pairs)
            step *= 2
        return x


def local(lat, dp, inputs, dec_bias, enc_weight, enc_bias, dec_weight, other_recon, active_blocks):
    grid = Grid(lat, dp)
    rows, width = inputs.shape
    lats = enc_weight.shape[1]
    block_size = lats // active_blocks.shape[1]
    f32, bf16 = jnp.float32, jnp.bfloat16
    bias = dec_bias.astype(f32)[None, :]
    x = inputs.astype(f32)
    centered_own = (x - bias).astype(bf16)
    centered = grid.gather(centered_own)
    planes = grid.planes

    pre_act = enc_bias[None, :]
    for k in range(planes):
        for m in range(4):
            w = lax.dynamic_slice(enc_weight, (grid.index(k, m) * width, 0), (width, lats))
            pre_act = pre_act + jnp.dot(centered[k][m], w, preferred_element_type=f32)
    gate = jnp.repeat(active_blocks.astype(f32), block_size, axis=1)
    positive = jnp.maximum(pre_act, 0.0)
    activations = (positive * positive * gate).astype(bf16)
    slope = positive * 2.0 * gate

    def dec_columns(k, m):
        return lax.dynamic_slice(dec_weight, (0, grid.index(k, m) * width), (lats, width))

    def part(k, m):
        return jnp.dot(activations, dec_columns(k, m), preferred_element_type=f32)

    recon = grid.scatter_sum(part)
    error_local = recon + (other_recon + bias) - x
    error = grid.gather(error_local.astype(bf16))
    squares = grid.total(jnp.broadcast_to(jnp.sum(error_local * error_local), (8, 128)))
    mse_loss = squares[0, 0] / (rows * dp * width * lat)

    dact = jnp.zeros((rows, lats), f32)
    grad_dec = jnp.zeros((lats, width * lat), f32)
    for k in range(planes):
        for m in range(4):
            e = error[k][m]
            g = lax.dot_general(activations, e, (((0,), (0,)), ((), ())), preferred_element_type=f32)
            grad_dec = lax.dynamic_update_slice(grad_dec, g, (0, grid.index(k, m) * width))
            dact = dact + lax.dot_general(
                e, dec_columns(k, m), (((1,), (1,)), ((), ())), preferred_element_type=f32
            )
    dpre = (dact * slope).astype(bf16)
    grad_enc = jnp.zeros((width * lat, lats), f32)
    for k in range(planes):
        for m in range(4):
            g = lax.dot_general(centered[k][m], dpre, (((0,), (0,)), ((), ())), preferred_element_type=f32)
            grad_enc = lax.dynamic_update_slice(grad_enc, g, (grid.index(k, m) * width, 0))
    grad_dec = lax.psum_scatter(grad_dec, "dp", scatter_dimension=0, tiled=True)
    grad_enc = lax.psum_scatter(grad_enc, "dp", scatter_dimension=1, tiled=True)
    return (error_local, mse_loss, grad_dec, grad_enc)


def solution(mesh):
    placed = (
        P("dp", "lat"),
        P("lat"),
        P(None, "lat"),
        P("lat"),
        P("lat", None),
        P("dp", "lat"),
        P("dp", "lat"),
    )
    lat, dp = mesh.shape["lat"], mesh.shape["dp"]

    def body(*args):
        return local(lat, dp, *args)

    return jax.shard_map(
        body,
        mesh=mesh,
        in_specs=placed,
        out_specs=(P("dp", "lat"), P(), P(("lat", "dp"), None), P(None, ("lat", "dp"))),
        check_vma=False,
    )
```

```python
import functools

import jax
import jax.numpy as jnp
from jax import lax
from jax.experimental import pallas as pl
from jax.experimental.pallas import tpu as pltpu
from jax.sharding import PartitionSpec as P


F32, BF16 = jnp.float32, jnp.bfloat16
VMEM_BYTES = 24 * 1024 * 1024
LANES = 128


def after(x, *earlier):
    return lax.optimization_barrier((x, *earlier))[0]


class Grid:
    def __init__(self, lat, dp):
        self.lat, self.dp, self.slots = lat, dp, lat // 4
        self.me = lax.axis_index("lat")
        self.rank = lax.axis_index("dp")
        first = jnp.where(self.rank % 2 == 0, 1, 2)
        members = jnp.stack([jnp.zeros_like(first), first, 3 - first, jnp.full_like(first, 3)])
        self.across = (0, 2, 1, 3) if dp == 2 else (0, 1, 2, 3)
        side = self.rank // (dp // 2)
        orders = [self.me ^ (4 * s + members) for s in range(self.slots)]
        self.order = [jnp.append(o, side).astype(jnp.int32) for o in orders]
        self.every = jnp.concatenate(orders).astype(jnp.int32)

    def swap(self, x, even, odd):
        pairs = []
        for i in range(self.lat):
            for d in range(self.dp):
                pairs.append((i * self.dp + d, (i ^ (even if d % 2 == 0 else odd)) * self.dp + d))
        return lax.ppermute(x, ("lat", "dp"), pairs)

    def swap_first(self, x):
        return self.swap(x, 1, 2)

    def swap_second(self, x):
        return self.swap(x, 2, 1)

    def swap_plane(self, x, bit):
        return self.swap(x, 4 * bit, 4 * bit)

    def swap_core(self, x):
        pairs = []
        for i in range(self.lat):
            for d in range(self.dp):
                pairs.append((i * self.dp + d, i * self.dp + (d ^ self.dp // 2)))
        return lax.ppermute(x, ("lat", "dp"), pairs)

    def spread(self, x, axis):
        h = self.dp // 4
        while h >= 1:
            bit = self.rank // h % 2
            size = x.shape[axis] // 2
            mine = lax.dynamic_slice_in_dim(x, bit * size, size, axis)
            other = lax.dynamic_slice_in_dim(x, (1 - bit) * size, size, axis)
            x = mine + lax.ppermute(other, "dp", [(d, d ^ h) for d in range(self.dp)])
            h //= 2
        return x

    def gather(self, own, use):
        column = [own]
        for s in range(1, self.slots):
            column.append(self.swap_plane(column[s & (s - 1)], s & -s))
        out, done = [], []
        last = self.slots - 1
        for s, block in enumerate(column):
            if s == 1 and last > 1:
                block = after(block, column[2], *out[0][1:])
            a = self.swap_first(block)
            b = self.swap_second(block)
            c = a
            if s == 1 < last:
                c = after(a, done[0])
            if s == 2 < last:
                c = after(a, column[3])
            if s == last > 2:
                c = after(a, done[1])
            out.append((block, a, b, self.swap_second(c)))
            done.append(use(s, out[-1]))
        return out

    def scatter_sum(self, part):
        column = [None] * self.slots
        earlier = {}
        got = None
        for s in reversed(range(self.slots)):
            keep, send = part(s, earlier.get(s))
            there = self.swap_second(send)
            pair = keep + there.astype(F32)
            other = pair[1].astype(BF16)
            got = self.swap_first(other if got is None else after(other, got))
            if s == self.slots - 1:
                earlier = {s - 2: there, s - 3: got}
            column[s] = pair[0] + got.astype(F32)
        for s in reversed(range(1, self.slots)):
            t = s & (s - 1)
            column[t] = column[t] + self.swap_plane(column[s].astype(BF16), s & -s).astype(F32)
        return column[0]


def plain(width):
    return width % LANES != 0


def taken(x, index, width, axis):
    return lax.dynamic_slice_in_dim(x, index * width, width, axis)


def gate_of(active, lats):
    rows, blocks = active.shape
    block = lats // blocks
    return jnp.concatenate(
        [jnp.broadcast_to(active[:, b:b + 1].astype(F32), (rows, block)) for b in range(blocks)], axis=1
    )


def activate(total, active):
    positive = jnp.maximum(total, 0.0)
    gated = positive * gate_of(active, total.shape[1])
    return (positive * gated).astype(BF16), 2.0 * gated


def outer(a, b):
    return lax.dot_general(a, b, (((0,), (0,)), ((), ())), preferred_element_type=F32)


def call(body, order, operands, in_specs, out_shape, out_specs, flops, moved, name, scratch=(), steps=1):
    return pl.pallas_call(
        body,
        grid_spec=pltpu.PrefetchScalarGridSpec(
            num_scalar_prefetch=1, grid=(steps,), in_specs=in_specs, out_specs=out_specs, scratch_shapes=scratch
        ),
        out_shape=out_shape,
        compiler_params=pltpu.CompilerParams(vmem_limit_bytes=VMEM_BYTES),
        cost_estimate=pl.CostEstimate(flops=flops, bytes_accessed=moved, transcendentals=0),
        name=name,
    )(order, *operands)


def whole(shape):
    return pl.BlockSpec(shape, lambda i, order: (0,) * len(shape))


def encode_body(last, order, x0, x1, x2, x3, w0, w1, w2, w3, acc, *rest):
    *rest, turned = rest
    width = x0.shape[1]
    total = acc[...]
    for m, (x, w) in enumerate(((x0, w0), (x1, w1), (x2, w2), (x3, w3))):
        total = total + jnp.dot(x[...], w[...], preferred_element_type=F32)
        turned[m * width:(m + 1) * width, :] = x[...].T
    if not last:
        rest[0][...] = total
        return
    active, act, slope = rest
    act[...], slope[...] = activate(total, active[...])


def encode(order, blocks, weight, acc, active):
    rows, width = blocks[0].shape
    lats = weight.shape[1]
    last = active is not None
    if plain(width):
        total = acc
        for m in range(4):
            total = total + jnp.dot(blocks[m], taken(weight, order[m], width, 0), preferred_element_type=F32)
        turned = jnp.concatenate([x.T for x in blocks], axis=0)
        return (*activate(total, active), turned) if last else (total, turned)
    row_specs = [
        pl.BlockSpec((width, lats), functools.partial(lambda m, i, order: (order[m], 0), m)) for m in range(4)
    ]
    operands = list(blocks) + [weight] * 4 + [acc]
    specs = [whole((rows, width))] * 4 + row_specs + [whole(acc.shape)]
    if last:
        operands.append(active)
        specs.append(whole(active.shape))
        out = [jax.ShapeDtypeStruct((rows, lats), BF16), jax.ShapeDtypeStruct((rows, lats), F32)]
    else:
        out = [jax.ShapeDtypeStruct((rows, lats), F32)]
    out.append(jax.ShapeDtypeStruct((4 * width, rows), BF16))
    return call(
        functools.partial(encode_body, last), order, operands, specs, out, [whole(o.shape) for o in out],
        8 * rows * width * lats, 8 * rows * width + 8 * width * lats + 8 * rows * lats, "encode",
    )


def column_specs(lats, width):
    return [pl.BlockSpec((lats, width), functools.partial(lambda m, i, order: (0, order[m]), m)) for m in range(4)]


def decode_body(order, act, w0, w1, w2, w3, keep, send):
    a = act[...]
    keep[0] = jnp.dot(a, w0[...], preferred_element_type=F32)
    keep[1] = jnp.dot(a, w1[...], preferred_element_type=F32)
    send[0] = jnp.dot(a, w2[...], preferred_element_type=F32).astype(BF16)
    send[1] = jnp.dot(a, w3[...], preferred_element_type=F32).astype(BF16)


def decode(order, act, weight, width):
    rows, lats = act.shape
    if plain(width):
        terms = [jnp.dot(act, taken(weight, order[m], width, 1), preferred_element_type=F32) for m in range(4)]
        return jnp.stack(terms[:2]), jnp.stack(terms[2:]).astype(BF16)
    out = [jax.ShapeDtypeStruct((2, rows, width), F32), jax.ShapeDtypeStruct((2, rows, width), BF16)]
    return call(
        decode_body, order, [act] + [weight] * 4, [whole(act.shape)] + column_specs(lats, width), out,
        [whole((2, rows, width))] * 2, 8 * rows * width * lats, 12 * rows * width + 8 * width * lats, "decode",
    )


def backward_body(last, across, order, act, e0, e1, e2, e3, w0, w1, w2, w3, dact, squares, *rest):
    rows, width = e0.shape
    half = act.shape[1] // 2
    total = dact[...]
    square = squares[...]
    if last:
        slope, grad_keep, grad_send, dpre_keep, dpre_send, next_squares = rest
    else:
        grad_keep, grad_send, next_dact, next_squares = rest
    side = order[order.shape[0] - 1]
    mine_at = pl.ds(pl.multiple_of(side * half, half), half)
    other_at = pl.ds(pl.multiple_of((1 - side) * half, half), half)
    mine, other = act[:, mine_at], act[:, other_at]
    for m, (e, w) in enumerate(((e0, w0), (e1, w1), (e2, w2), (e3, w3))):
        block = e[...]
        total = total + lax.dot_general(block, w[...], (((1,), (1,)), ((), ())), preferred_element_type=F32)
        wide = block.astype(F32)
        square = square + jnp.sum((wide * wide).reshape(rows // 8, 8, width), axis=0)
        at, there = pl.ds(m * width, width), pl.ds(across[m] * width, width)
        grad_keep[:, at] = lax.dot_general(mine, block, (((0,), (0,)), ((), ())), preferred_element_type=F32)
        grad_send[:, there] = lax.dot_general(
            other, block, (((0,), (0,)), ((), ())), preferred_element_type=F32
        ).astype(BF16)
    if last:
        next_squares[...] = jnp.broadcast_to(jnp.sum(square, axis=(0, 1), keepdims=True), next_squares.shape)
        slope[...] = total * slope[...]
        dpre_keep[...] = slope[:, mine_at].astype(BF16)
        dpre_send[...] = slope[:, other_at].astype(BF16)
    else:
        next_dact[...] = total
        next_squares[...] = square


def backward(order, across, act, blocks, weight, dact, squares, slope):
    rows, width = blocks[0].shape
    lats = act.shape[1]
    last = slope is not None
    if plain(width):
        half, side = lats // 2, order[-1]
        mine, other = taken(act, side, half, 1), taken(act, 1 - side, half, 1)
        for e, m in zip(blocks, range(4)):
            w = taken(weight, order[m], width, 1)
            dact = dact + lax.dot_general(e, w, (((1,), (1,)), ((), ())), preferred_element_type=F32)
            squares = squares + jnp.sum(e.astype(F32) ** 2) / squares.size
        keep = jnp.concatenate([outer(mine, e) for e in blocks], axis=1)
        send = jnp.concatenate([outer(other, blocks[m]) for m in across], axis=1).astype(BF16)
        if not last:
            return keep, send, dact, squares
        dpre = (dact * slope).astype(BF16)
        squares = jnp.broadcast_to(jnp.sum(squares), (8, LANES))
        return keep, send, taken(dpre, side, half, 1), taken(dpre, 1 - side, half, 1), squares
    operands = [act] + list(blocks) + [weight] * 4 + [dact, squares]
    specs = [whole(act.shape)] + [whole((rows, width))] * 4 + column_specs(lats, width)
    specs += [whole(dact.shape), whole(squares.shape)]
    if last:
        operands.append(slope)
        specs.append(whole(slope.shape))
    out = [
        jax.ShapeDtypeStruct((lats // 2, 4 * width), F32),
        jax.ShapeDtypeStruct((lats // 2, 4 * width), BF16),
    ]
    if last:
        out += [jax.ShapeDtypeStruct((rows, lats // 2), BF16)] * 2
    else:
        out.append(jax.ShapeDtypeStruct((rows, lats), F32))
    out.append(jax.ShapeDtypeStruct((8, 128) if last else squares.shape, F32))
    return call(
        functools.partial(backward_body, last, across), order, operands, specs, out, [whole(o.shape) for o in out],
        16 * rows * width * lats, 8 * rows * width + 20 * width * lats + 8 * rows * lats, "backward",
    )


def decoder_gradient_body(slots, width, order, *refs):
    keeps, gots, out = refs[:slots], refs[slots:2 * slots], refs[-1]
    for s in range(slots):
        for m in range(4):
            at = pl.ds(m * width, width)
            there = pl.ds(pl.multiple_of(order[4 * s + m] * width, width), width)
            out[:, there] = keeps[s][:, at] + gots[s][:, at].astype(F32)


def decoder_gradient(order, keeps, gots, width):
    slots = len(keeps)
    half = keeps[0].shape[0]
    operands = keeps + gots
    size = half * 4 * slots * width
    if plain(width):
        out = jnp.zeros((half, 4 * slots * width), F32)
        for s in range(slots):
            part = keeps[s] + gots[s].astype(F32)
            for m in range(4):
                block = part[:, m * width:(m + 1) * width]
                out = lax.dynamic_update_slice_in_dim(out, block, order[4 * s + m] * width, 1)
        return out
    return call(
        functools.partial(decoder_gradient_body, slots, width), order, operands, [whole(o.shape) for o in operands],
        jax.ShapeDtypeStruct((half, 4 * slots * width), F32), whole((half, 4 * slots * width)), size, 10 * size,
        "decoder_gradient",
    )


def encoder_gradient_body(slots, width, across, order, *refs):
    mine, theirs = refs[:slots], refs[slots:2 * slots]
    dpre, got, out = refs[2 * slots:]
    d, g = dpre[...], got[...]
    for s in range(slots):
        for m in range(4):
            here = jnp.dot(mine[s][m * width:(m + 1) * width, :], d, preferred_element_type=F32)
            at = across[m] * width
            here += jnp.dot(theirs[s][at:at + width, :], g, preferred_element_type=F32)
            out[pl.ds(pl.multiple_of(order[4 * s + m] * width, width), width), :] = here


def encoder_gradient(order, across, mine, theirs, dpre, got, width):
    slots = len(mine)
    rows, half = dpre.shape
    operands = mine + theirs + [dpre, got]
    shape = (4 * slots * width, half)
    if plain(width):
        out = jnp.zeros(shape, F32)
        for s in range(slots):
            for m in range(4):
                a, b = m * width, across[m] * width
                block = jnp.dot(mine[s][a:a + width], dpre, preferred_element_type=F32)
                block += jnp.dot(theirs[s][b:b + width], got, preferred_element_type=F32)
                out = lax.dynamic_update_slice_in_dim(out, block, order[4 * s + m] * width, 0)
        return out
    return call(
        functools.partial(encoder_gradient_body, slots, width, across), order, operands,
        [whole(o.shape) for o in operands], jax.ShapeDtypeStruct(shape, F32), whole(shape),
        4 * shape[0] * rows * half, 4 * shape[0] * rows + 4 * shape[0] * half, "encoder_gradient",
    )


def local(lat, dp, inputs, dec_bias, enc_weight, enc_bias, dec_weight, other_recon, active_blocks):
    grid = Grid(lat, dp)
    rows, width = inputs.shape
    lats = enc_weight.shape[1]
    half = lats // 2
    slots = grid.slots
    bias = dec_bias.astype(F32)[None, :]
    x = inputs.astype(F32)
    sums = [enc_bias[None, :]]

    def enter(s, blocks):
        *sums[:], mine = encode(grid.order[s], blocks, enc_weight, sums[0], active_blocks if s == slots - 1 else None)
        turned.append(mine)
        return sums[0]

    turned = []
    grid.gather((x - bias).astype(BF16), enter)
    act, slope = sums
    theirs = [grid.swap_core(t) for t in turned]

    def part(s, earlier):
        wait = [] if earlier is None else [earlier]
        if s == 0:
            wait += theirs
        return decode(grid.order[s], after(act, *wait) if wait else act, dec_weight, width)

    recon = grid.scatter_sum(part)
    bias, x = (a.astype(F32) for a in lax.optimization_barrier((dec_bias, inputs, act))[:2])
    error_local = recon + (other_recon + bias[None, :]) - x
    state = [jnp.zeros((rows, lats), F32), jnp.zeros((8, width), F32)]
    keeps, gots = [], []

    def back(s, blocks):
        order = grid.order[s]
        if s >= 2:
            state[0] = after(state[0], gots[s - 2])
        keep, send, *state[:] = backward(
            order, grid.across, act, blocks, dec_weight, *state, slope if s == slots - 1 else None
        )
        keeps.append(keep)
        gots.append(grid.swap_core(send))
        return state[0]

    grid.gather(error_local.astype(BF16), back)
    mine, other, squares = state

    got = grid.swap_core(other)
    grad_dec = decoder_gradient(grid.every, keeps, gots, width)
    grad_enc = encoder_gradient(grid.every, grid.across, turned, theirs, mine, after(got, grad_dec), width)

    square = squares
    step = 1
    while step < dp:
        square = square + lax.ppermute(square, "dp", [(d, d ^ step) for d in range(dp)])
        step *= 2
    mse_loss = square[0, 0] / (rows * dp * width * lat)
    return (error_local, mse_loss, grid.spread(grad_dec, 0), grid.spread(grad_enc, 1))


def solution(mesh):
    placed = (
        P("dp", "lat"),
        P("lat"),
        P(None, "lat"),
        P("lat"),
        P("lat", None),
        P("dp", "lat"),
        P("dp", "lat"),
    )
    lat, dp = mesh.shape["lat"], mesh.shape["dp"]
    return jax.shard_map(
        functools.partial(local, lat, dp),
        mesh=mesh,
        in_specs=placed,
        out_specs=(P("dp", "lat"), P(), P(("lat", "dp"), None), P(None, ("lat", "dp"))),
        check_vma=False,
    )
```

```python
import functools

import jax
import jax.numpy as jnp
from jax import lax
from jax.experimental import pallas as pl
from jax.experimental.pallas import tpu as pltpu
from jax.sharding import PartitionSpec as P


F32, BF16 = jnp.float32, jnp.bfloat16
VMEM_BYTES = 24 * 1024 * 1024
LANES = 128


class Grid:
    def __init__(self, lat, dp):
        self.lat, self.dp, self.slots = lat, dp, lat // 4
        self.me = lax.axis_index("lat")
        self.rank = lax.axis_index("dp")
        first = jnp.where(self.rank % 2 == 0, 1, 2)
        members = jnp.stack([jnp.zeros_like(first), first, 3 - first, jnp.full_like(first, 3)])
        self.across = (0, 2, 1, 3) if dp == 2 else (0, 1, 2, 3)
        side = self.rank // (dp // 2)
        orders = [self.me ^ (4 * s + members) for s in range(self.slots)]
        self.order = [jnp.append(o, side).astype(jnp.int32) for o in orders]
        self.every = jnp.concatenate(orders).astype(jnp.int32)

    def swap(self, x, even, odd):
        pairs = []
        for i in range(self.lat):
            for d in range(self.dp):
                pairs.append((i * self.dp + d, (i ^ (even if d % 2 == 0 else odd)) * self.dp + d))
        return lax.ppermute(x, ("lat", "dp"), pairs)

    def swap_first(self, x):
        return self.swap(x, 1, 2)

    def swap_second(self, x):
        return self.swap(x, 2, 1)

    def swap_plane(self, x, bit):
        return self.swap(x, 4 * bit, 4 * bit)

    def swap_core(self, x):
        pairs = []
        for i in range(self.lat):
            for d in range(self.dp):
                pairs.append((i * self.dp + d, i * self.dp + (d ^ self.dp // 2)))
        return lax.ppermute(x, ("lat", "dp"), pairs)

    def spread(self, x, axis):
        h = self.dp // 4
        while h >= 1:
            bit = self.rank // h % 2
            size = x.shape[axis] // 2
            mine = lax.dynamic_slice_in_dim(x, bit * size, size, axis)
            other = lax.dynamic_slice_in_dim(x, (1 - bit) * size, size, axis)
            x = mine + lax.ppermute(other, "dp", [(d, d ^ h) for d in range(self.dp)])
            h //= 2
        return x

    def gather(self, own):
        column = [own]
        for s in range(1, self.slots):
            column.append(self.swap_plane(column[s & (s - 1)], s & -s))
        seconds = []
        for s, block in enumerate(column):
            seconds.append(self.swap_plane(seconds[-1], 1) if s % 2 else self.swap_first(block))
        return [(b, a, self.swap_second(b), self.swap_second(a)) for b, a in zip(column, seconds)]

    def scatter_sum(self, part):
        column = [None] * self.slots
        earlier = {}
        last = self.slots - 1
        moved = None
        for s in reversed(range(self.slots)):
            keep, send = part(s, earlier.get(s))
            there = self.swap_second(send)
            pair = keep + there.astype(F32)
            if s == last > 1:
                other = self.swap_plane(pair[1].astype(BF16), 1)
                moved = (self.swap_plane(pair[0].astype(BF16), 1), other)
                earlier = {s - 2: there, s - 3: other}
                continue
            mine, other = pair[0], pair[1]
            if s == last - 1:
                mine, other = mine + moved[0].astype(F32), other + moved[1].astype(F32)
            got = self.swap_first(other.astype(BF16))
            column[s] = mine + got.astype(F32)
        for s in reversed(range(1, self.slots)):
            if column[s] is not None:
                t = s & (s - 1)
                send = column[s].astype(BF16)
                column[t] = column[t] + self.swap_plane(send, s & -s).astype(F32)
        return column[0]


def plain(width):
    return width % LANES != 0


def taken(x, index, width, axis):
    return lax.dynamic_slice_in_dim(x, index * width, width, axis)


def gate_of(active, lats):
    blocks, rows = active.shape
    turned = active.astype(F32).T
    return jnp.concatenate(
        [jnp.broadcast_to(turned[:, b:b + 1], (rows, lats // blocks)) for b in range(blocks)], axis=1
    )


def activate(total, active):
    positive = jnp.maximum(total, 0.0)
    gated = positive * gate_of(active, total.shape[1])
    return (positive * gated).astype(BF16), 2.0 * gated


def outer(a, b):
    return lax.dot_general(a, b, (((0,), (0,)), ((), ())), preferred_element_type=F32)


def call(body, order, operands, in_specs, out_shape, out_specs, flops, moved, name, scratch=()):
    return pl.pallas_call(
        body,
        grid_spec=pltpu.PrefetchScalarGridSpec(
            num_scalar_prefetch=1, grid=(1,), in_specs=in_specs, out_specs=out_specs, scratch_shapes=scratch
        ),
        out_shape=out_shape,
        compiler_params=pltpu.CompilerParams(vmem_limit_bytes=VMEM_BYTES),
        cost_estimate=pl.CostEstimate(flops=flops, bytes_accessed=moved, transcendentals=0),
        name=name,
    )(order, *operands)


ANYWHERE = pl.BlockSpec(memory_space=pl.ANY)
FAR = pl.BlockSpec(memory_space=pltpu.HBM)


def whole(shape):
    return pl.BlockSpec(shape, lambda i, order: (0,) * len(shape))


def encode_body(count, last, order, *refs):
    xs, (weight, start, *refs) = refs[:count], refs[count:]
    width = xs[0].shape[1]
    if last:
        active, act, slope, held, rows_of, begun, gates, sems = refs
        pairs = [(active, gates)]
    else:
        total_out, held, rows_of, begun, sems = refs
        pairs = []
    pairs.append((start, begun))
    for b in range(count):
        at = pl.ds(pl.multiple_of(order[b] * width, width), width)
        pairs += [(xs[b], held.at[b]), (weight.at[at], rows_of.at[b])]
    loads = [pltpu.make_async_copy(a, b, sems.at[n]) for n, (a, b) in enumerate(pairs)]
    for load in loads:
        load.start()
    for load in loads[:-2 * count]:
        load.wait()
    total = begun[...]
    for b in range(count):
        loads[2 * (b - count)].wait()
        loads[2 * (b - count) + 1].wait()
        total = total + jnp.dot(held[b], rows_of[b], preferred_element_type=F32)
    if last:
        act[...], slope[...] = activate(total, gates[...])
    else:
        total_out[...] = total


def encode(order, blocks, weight, start, active):
    count = len(blocks)
    rows, width = blocks[0].shape
    lats = weight.shape[1]
    last = active is not None
    if plain(width):
        total = start
        for b in range(count):
            total = total + jnp.dot(blocks[b], taken(weight, order[b], width, 0), preferred_element_type=F32)
        return activate(total, active) if last else [total]
    out = [jax.ShapeDtypeStruct((rows, lats), F32)]
    operands = blocks + [weight, start]
    scratch = [pltpu.VMEM((count, rows, width), BF16), pltpu.VMEM((count, width, lats), BF16)]
    scratch.append(pltpu.VMEM(start.shape, F32))
    if last:
        out = [jax.ShapeDtypeStruct((rows, lats), BF16)] + out
        operands.append(active)
        scratch.append(pltpu.VMEM(active.shape, active.dtype))
    scratch.append(pltpu.SemaphoreType.DMA((2 * count + 2,)))
    return call(
        functools.partial(encode_body, count, last), order, operands, [FAR] * len(operands), out,
        [whole(o.shape) for o in out],
        2 * count * rows * width * lats, 2 * count * width * (rows + lats) + 8 * rows * lats, "encode", scratch,
    )


def bring_body(order, x, out, sem):
    copy = pltpu.make_async_copy(x, out, sem)
    copy.start()
    copy.wait()


def bring(order, x):
    return call(
        bring_body, order, [x], [FAR], jax.ShapeDtypeStruct(x.shape, x.dtype),
        pl.BlockSpec(memory_space=pltpu.VMEM), 0, 4 * x.size, "bring", [pltpu.SemaphoreType.DMA],
    )


def turn_body(count, order, *refs):
    xs, (out, held, turned, in_sems, out_sems) = refs[:count], refs[count:]
    width = held.shape[2]
    loads = [pltpu.make_async_copy(xs[b], held.at[b], in_sems.at[b]) for b in range(count)]
    for load in loads:
        load.start()
    stores = []
    for b in range(count):
        loads[b].wait()
        turned[b] = held[b].T
        stores.append(pltpu.make_async_copy(turned.at[b], out.at[b], out_sems.at[b]))
        stores[-1].start()
    for store in stores:
        store.wait()


def turn(order, blocks):
    count = len(blocks)
    rows, width = blocks[0].shape
    if plain(width):
        return jnp.stack([x.T for x in blocks])
    shape = (count, width, rows)
    return call(
        functools.partial(turn_body, count), order, blocks, [FAR] * count, jax.ShapeDtypeStruct(shape, BF16), FAR,
        0, 4 * count * rows * width, "turn",
        [pltpu.VMEM((count, rows, width), BF16), pltpu.VMEM(shape, BF16),
         pltpu.SemaphoreType.DMA((count,)), pltpu.SemaphoreType.DMA((count,))],
    )


def column_specs(lats, width):
    return [pl.BlockSpec((lats, width), functools.partial(lambda m, i, order: (0, order[m]), m)) for m in range(4)]


def decode_body(order, act, w0, w1, w2, w3, *rest):
    *_, keep, send = rest
    a = act[...]
    keep[0] = jnp.dot(a, w0[...], preferred_element_type=F32)
    keep[1] = jnp.dot(a, w1[...], preferred_element_type=F32)
    send[0] = jnp.dot(a, w2[...], preferred_element_type=F32).astype(BF16)
    send[1] = jnp.dot(a, w3[...], preferred_element_type=F32).astype(BF16)


def decode(order, act, weight, width, earlier):
    rows, lats = act.shape
    if plain(width):
        terms = [jnp.dot(act, taken(weight, order[m], width, 1), preferred_element_type=F32) for m in range(4)]
        return jnp.stack(terms[:2]), jnp.stack(terms[2:]).astype(BF16)
    out = [jax.ShapeDtypeStruct((2, rows, width), F32), jax.ShapeDtypeStruct((2, rows, width), BF16)]
    return call(
        decode_body, order, [act] + [weight] * 4 + earlier,
        [whole(act.shape)] + column_specs(lats, width) + [ANYWHERE] * len(earlier), out,
        [whole((2, rows, width))] * 2, 8 * rows * width * lats, 12 * rows * width + 8 * width * lats, "decode",
    )


def backward_body(last, across, order, act, e0, e1, e2, e3, w0, w1, w2, w3, dact, squares, *rest):
    rows, width = e0.shape
    half = act.shape[1] // 2
    total = dact[...]
    square = squares[...]
    if last:
        slope, grad_keep, grad_send, dpre_keep, dpre_send, next_squares = rest
    else:
        grad_keep, grad_send, next_dact, next_squares = rest
    side = order[order.shape[0] - 1]
    mine_at = pl.ds(pl.multiple_of(side * half, half), half)
    other_at = pl.ds(pl.multiple_of((1 - side) * half, half), half)
    mine, other = act[:, mine_at], act[:, other_at]
    for m, (e, w) in enumerate(((e0, w0), (e1, w1), (e2, w2), (e3, w3))):
        block = e[...]
        total = total + lax.dot_general(block, w[...], (((1,), (1,)), ((), ())), preferred_element_type=F32)
        wide = block.astype(F32)
        square = square + jnp.sum((wide * wide).reshape(rows // 8, 8, width), axis=0)
        at, there = pl.ds(m * width, width), pl.ds(across[m] * width, width)
        grad_keep[:, at] = lax.dot_general(mine, block, (((0,), (0,)), ((), ())), preferred_element_type=F32)
        grad_send[:, there] = lax.dot_general(
            other, block, (((0,), (0,)), ((), ())), preferred_element_type=F32
        ).astype(BF16)
    if last:
        next_squares[...] = jnp.broadcast_to(jnp.sum(square, axis=(0, 1), keepdims=True), next_squares.shape)
        slope[...] = total * slope[...]
        dpre_keep[...] = slope[:, mine_at].astype(BF16)
        dpre_send[...] = slope[:, other_at].astype(BF16)
    else:
        next_dact[...] = total
        next_squares[...] = square


def backward(order, across, act, blocks, weight, dact, squares, slope):
    rows, width = blocks[0].shape
    lats = act.shape[1]
    last = slope is not None
    if plain(width):
        half, side = lats // 2, order[-1]
        mine, other = taken(act, side, half, 1), taken(act, 1 - side, half, 1)
        for e, m in zip(blocks, range(4)):
            w = taken(weight, order[m], width, 1)
            dact = dact + lax.dot_general(e, w, (((1,), (1,)), ((), ())), preferred_element_type=F32)
            squares = squares + jnp.sum(e.astype(F32) ** 2) / squares.size
        keep = jnp.concatenate([outer(mine, e) for e in blocks], axis=1)
        send = jnp.concatenate([outer(other, blocks[m]) for m in across], axis=1).astype(BF16)
        if not last:
            return keep, send, dact, squares
        dpre = (dact * slope).astype(BF16)
        squares = jnp.broadcast_to(jnp.sum(squares), (8, LANES))
        return keep, send, taken(dpre, side, half, 1), taken(dpre, 1 - side, half, 1), squares
    operands = [act] + list(blocks) + [weight] * 4 + [dact, squares]
    specs = [whole(act.shape)] + [whole((rows, width))] * 4 + column_specs(lats, width)
    specs += [whole(dact.shape), whole(squares.shape)]
    if last:
        operands.append(slope)
        specs.append(whole(slope.shape))
    out = [
        jax.ShapeDtypeStruct((lats // 2, 4 * width), F32),
        jax.ShapeDtypeStruct((lats // 2, 4 * width), BF16),
    ]
    if last:
        out += [jax.ShapeDtypeStruct((rows, lats // 2), BF16)] * 2
    else:
        out.append(jax.ShapeDtypeStruct((rows, lats), F32))
    out.append(jax.ShapeDtypeStruct((8, 128) if last else squares.shape, F32))
    return call(
        functools.partial(backward_body, last, across), order, operands, specs, out, [whole(o.shape) for o in out],
        16 * rows * width * lats, 8 * rows * width + 20 * width * lats + 8 * rows * lats, "backward",
    )


def decoder_gradient_body(slots, width, scale, order, *refs):
    keeps, gots, (square, square_got, out, mean) = refs[:slots], refs[slots:2 * slots], refs[2 * slots:]
    mean[...] = (square[0:1, 0:1] + square_got[0:1, 0:1]) * scale
    for s in range(slots):
        for m in range(4):
            at = pl.ds(m * width, width)
            there = pl.ds(pl.multiple_of(order[4 * s + m] * width, width), width)
            out[:, there] = keeps[s][:, at] + gots[s][:, at].astype(F32)


def decoder_gradient(order, keeps, gots, width, squares, count):
    slots = len(keeps)
    half = keeps[0].shape[0]
    operands = keeps + gots + list(squares)
    size = half * 4 * slots * width
    if plain(width):
        out = jnp.zeros((half, 4 * slots * width), F32)
        for s in range(slots):
            part = keeps[s] + gots[s].astype(F32)
            for m in range(4):
                block = part[:, m * width:(m + 1) * width]
                out = lax.dynamic_update_slice_in_dim(out, block, order[4 * s + m] * width, 1)
        return out, (squares[0] + squares[1])[:1, :1] / count
    return call(
        functools.partial(decoder_gradient_body, slots, width, 1.0 / count), order, operands,
        [whole(o.shape) for o in operands],
        [jax.ShapeDtypeStruct((half, 4 * slots * width), F32), jax.ShapeDtypeStruct((1, 1), F32)],
        [whole((half, 4 * slots * width)), whole((1, 1))], size, 10 * size,
        "decoder_gradient",
    )


def encoder_send_body(slots, width, across, order, mine, dpre, out):
    d = dpre[...]
    for s in range(slots):
        for m in range(4):
            here = jnp.dot(mine[4 * s + m], d, preferred_element_type=F32)
            at = (4 * s + across[m]) * width
            out[at:at + width, :] = here.astype(BF16)


def encoder_send(order, across, mine, dpre, width):
    slots = mine.shape[0] // 4
    rows, half = dpre.shape
    operands = [mine, dpre]
    shape = (4 * slots * width, half)
    if plain(width):
        blocks = [mine[4 * s + m] for s in range(slots) for m in across]
        return jnp.dot(jnp.concatenate(blocks), dpre, preferred_element_type=F32).astype(BF16)
    return call(
        functools.partial(encoder_send_body, slots, width, across), order, operands,
        [whole(o.shape) for o in operands], jax.ShapeDtypeStruct(shape, BF16), whole(shape),
        2 * shape[0] * rows * half, 2 * shape[0] * rows + 2 * shape[0] * half, "encoder_send",
    )


def encoder_gradient_body(slots, width, order, mine, dpre, got, out):
    d = dpre[...]
    for s in range(slots):
        for m in range(4):
            here = jnp.dot(mine[4 * s + m], d, preferred_element_type=F32)
            at = (4 * s + m) * width
            there = pl.ds(pl.multiple_of(order[4 * s + m] * width, width), width)
            out[there, :] = here + got[at:at + width, :].astype(F32)


def encoder_gradient(order, mine, dpre, got, width):
    slots = mine.shape[0] // 4
    rows, half = dpre.shape
    operands = [mine, dpre, got]
    shape = (4 * slots * width, half)
    if plain(width):
        out = jnp.zeros(shape, F32)
        total = jnp.dot(mine.reshape(shape[0], rows), dpre, preferred_element_type=F32) + got.astype(F32)
        for b in range(4 * slots):
            out = lax.dynamic_update_slice_in_dim(out, total[b * width:(b + 1) * width], order[b] * width, 0)
        return out
    return call(
        functools.partial(encoder_gradient_body, slots, width), order, operands,
        [whole(o.shape) for o in operands], jax.ShapeDtypeStruct(shape, F32), whole(shape),
        2 * shape[0] * rows * half, 2 * shape[0] * rows + 6 * shape[0] * half, "encoder_gradient",
    )


def local(lat, dp, inputs, dec_bias, enc_weight, enc_bias, dec_weight, other_recon, active_blocks):
    grid = Grid(lat, dp)
    rows, width = inputs.shape
    lats = enc_weight.shape[1]
    half = lats // 2
    slots = grid.slots
    centered = grid.gather((inputs.astype(F32) - dec_bias.astype(F32)[None, :]).astype(BF16))
    centered = [block for slot in centered for block in slot]
    near = dec_weight if plain(width) else bring(grid.every, dec_weight)
    (pre_act,) = encode(grid.every[:-4], centered[:-4], enc_weight, enc_bias[None, :], None)
    act, slope = encode(grid.every[-4:], centered[-4:], enc_weight, pre_act, active_blocks.T)
    turned = turn(grid.every, centered)

    def part(s, earlier):
        earlier = [] if earlier is None else [earlier]
        if s == slots // 2 - 1:
            earlier.append(turned)
        return decode(grid.order[s], act, near, width, earlier)

    recon = grid.scatter_sum(part)
    bias, x = dec_bias.astype(F32), inputs.astype(F32)
    error_local = recon + (other_recon + bias[None, :]) - x
    state = [jnp.zeros((rows, lats), F32), jnp.zeros((8, width), F32)]
    keeps, gots = [], []

    for s, blocks in enumerate(grid.gather(error_local.astype(BF16))):
        order = grid.order[s]
        keep, send, *state[:] = backward(
            order, grid.across, act, blocks, near, *state, slope if s == slots - 1 else None
        )
        keeps.append(keep)
        gots.append(grid.swap_core(send))

    mine, other, squares = state

    square, step = squares, 1
    while step < dp:
        square_got = lax.ppermute(square, "dp", [(d, d ^ step) for d in range(dp)])
        step *= 2
        if step < dp:
            square = square + square_got
    got = grid.swap_core(encoder_send(grid.every, grid.across, turned, other, width))
    grad_dec, mean = decoder_gradient(
        grid.every, keeps, gots, width, (square, square_got), rows * dp * width * lat
    )
    mse_loss = mean.reshape(())
    grad_enc = encoder_gradient(grid.every, turned, mine, got, width)

    return (error_local, mse_loss, grid.spread(grad_dec, 0), grid.spread(grad_enc, 1))


def solution(mesh):
    placed = (
        P("dp", "lat"),
        P("lat"),
        P(None, "lat"),
        P("lat"),
        P("lat", None),
        P("dp", "lat"),
        P("dp", "lat"),
    )
    lat, dp = mesh.shape["lat"], mesh.shape["dp"]
    return jax.shard_map(
        functools.partial(local, lat, dp),
        mesh=mesh,
        in_specs=placed,
        out_specs=(P("dp", "lat"), P(), P(("lat", "dp"), None), P(None, ("lat", "dp"))),
        check_vma=False,
    )
```

```python
import functools

import jax
import jax.numpy as jnp
from jax import lax
from jax.experimental import pallas as pl
from jax.experimental.pallas import tpu as pltpu
from jax.sharding import PartitionSpec as P


F32, BF16 = jnp.float32, jnp.bfloat16
VMEM_BYTES = 24 * 1024 * 1024
LANES = 128


class Grid:
    def __init__(self, lat, dp):
        self.lat, self.dp, self.slots = lat, dp, lat // 4
        self.me = lax.axis_index("lat")
        self.rank = lax.axis_index("dp")
        first = jnp.where(self.rank % 2 == 0, 1, 2)
        members = jnp.stack([jnp.zeros_like(first), first, 3 - first, jnp.full_like(first, 3)])
        self.across = (0, 2, 1, 3) if dp == 2 else (0, 1, 2, 3)
        side = self.rank // (dp // 2)
        orders = [self.me ^ (4 * s + members) for s in range(self.slots)]
        self.order = [jnp.append(o, side).astype(jnp.int32) for o in orders]
        self.every = jnp.concatenate(orders).astype(jnp.int32)

    def swap(self, x, even, odd):
        pairs = []
        for i in range(self.lat):
            for d in range(self.dp):
                pairs.append((i * self.dp + d, (i ^ (even if d % 2 == 0 else odd)) * self.dp + d))
        return lax.ppermute(x, ("lat", "dp"), pairs)

    def swap_first(self, x):
        return self.swap(x, 1, 2)

    def swap_second(self, x):
        return self.swap(x, 2, 1)

    def swap_plane(self, x, bit):
        return self.swap(x, 4 * bit, 4 * bit)

    def swap_core(self, x):
        pairs = []
        for i in range(self.lat):
            for d in range(self.dp):
                pairs.append((i * self.dp + d, i * self.dp + (d ^ self.dp // 2)))
        return lax.ppermute(x, ("lat", "dp"), pairs)

    def spread(self, x, axis):
        h = self.dp // 4
        while h >= 1:
            bit = self.rank // h % 2
            size = x.shape[axis] // 2
            mine = lax.dynamic_slice_in_dim(x, bit * size, size, axis)
            other = lax.dynamic_slice_in_dim(x, (1 - bit) * size, size, axis)
            x = mine + lax.ppermute(other, "dp", [(d, d ^ h) for d in range(self.dp)])
            h //= 2
        return x

    def gather(self, own):
        column = [own]
        for s in range(1, self.slots):
            column.append(self.swap_plane(column[s & (s - 1)], s & -s))
        seconds = []
        for s, block in enumerate(column):
            seconds.append(self.swap_plane(seconds[-1], 1) if s % 2 else self.swap_first(block))
        return [(b, a, self.swap_second(b), self.swap_second(a)) for b, a in zip(column, seconds)]

    def scatter_sum(self, part):
        column = [None] * self.slots
        earlier = {}
        last = self.slots - 1
        moved = None
        for s in reversed(range(self.slots)):
            keep, send = part(s, earlier.get(s))
            there = self.swap_second(send)
            pair = keep + there.astype(F32)
            if s == last > 1:
                other = self.swap_plane(pair[1].astype(BF16), 1)
                moved = (self.swap_plane(pair[0].astype(BF16), 1), other)
                earlier = {s - 2: there, s - 3: other}
                continue
            mine, other = pair[0], pair[1]
            if s == last - 1:
                mine, other = mine + moved[0].astype(F32), other + moved[1].astype(F32)
            got = self.swap_first(other.astype(BF16))
            column[s] = mine + got.astype(F32)
        for s in reversed(range(1, self.slots)):
            if column[s] is not None:
                t = s & (s - 1)
                send = column[s].astype(BF16)
                column[t] = column[t] + self.swap_plane(send, s & -s).astype(F32)
        return column[0]


def plain(width):
    return width % LANES != 0


def taken(x, index, width, axis):
    return lax.dynamic_slice_in_dim(x, index * width, width, axis)


def gate_of(active, lats):
    blocks, rows = active.shape
    turned = active.astype(F32).T
    return jnp.concatenate(
        [jnp.broadcast_to(turned[:, b:b + 1], (rows, lats // blocks)) for b in range(blocks)], axis=1
    )


def activate(total, active):
    positive = jnp.maximum(total, 0.0)
    gated = positive * gate_of(active, total.shape[1])
    return (positive * gated).astype(BF16), 2.0 * gated


def outer(a, b):
    return lax.dot_general(a, b, (((0,), (0,)), ((), ())), preferred_element_type=F32)


def call(body, order, operands, in_specs, out_shape, out_specs, flops, moved, name, scratch=()):
    return pl.pallas_call(
        body,
        grid_spec=pltpu.PrefetchScalarGridSpec(
            num_scalar_prefetch=1, grid=(1,), in_specs=in_specs, out_specs=out_specs, scratch_shapes=scratch
        ),
        out_shape=out_shape,
        compiler_params=pltpu.CompilerParams(vmem_limit_bytes=VMEM_BYTES),
        cost_estimate=pl.CostEstimate(flops=flops, bytes_accessed=moved, transcendentals=0),
        name=name,
    )(order, *operands)


ANYWHERE = pl.BlockSpec(memory_space=pl.ANY)
FAR = pl.BlockSpec(memory_space=pltpu.HBM)


def whole(shape):
    return pl.BlockSpec(shape, lambda i, order: (0,) * len(shape))


def encode_body(count, last, order, *refs):
    xs, (weight, start, *refs) = refs[:count], refs[count:]
    width = xs[0].shape[1]
    if last:
        active, act, slope, held, rows_of, begun, gates, sems = refs
        pairs = [(active, gates)]
    else:
        total_out, held, rows_of, begun, sems = refs
        pairs = []
    pairs.append((start, begun))
    for b in range(count):
        at = pl.ds(pl.multiple_of(order[b] * width, width), width)
        pairs += [(xs[b], held.at[b]), (weight.at[at], rows_of.at[b])]
    loads = [pltpu.make_async_copy(a, b, sems.at[n]) for n, (a, b) in enumerate(pairs)]
    for load in loads:
        load.start()
    for load in loads[:-2 * count]:
        load.wait()
    total = begun[...]
    for b in range(count):
        loads[2 * (b - count)].wait()
        loads[2 * (b - count) + 1].wait()
        total = total + jnp.dot(held[b], rows_of[b], preferred_element_type=F32)
    if last:
        act[...], slope[...] = activate(total, gates[...])
    else:
        total_out[...] = total


def encode(order, blocks, weight, start, active):
    count = len(blocks)
    rows, width = blocks[0].shape
    lats = weight.shape[1]
    last = active is not None
    if plain(width):
        total = start
        for b in range(count):
            total = total + jnp.dot(blocks[b], taken(weight, order[b], width, 0), preferred_element_type=F32)
        return activate(total, active) if last else [total]
    out = [jax.ShapeDtypeStruct((rows, lats), F32)]
    operands = blocks + [weight, start]
    scratch = [pltpu.VMEM((count, rows, width), BF16), pltpu.VMEM((count, width, lats), BF16)]
    scratch.append(pltpu.VMEM(start.shape, F32))
    if last:
        out = [jax.ShapeDtypeStruct((rows, lats), BF16)] + out
        operands.append(active)
        scratch.append(pltpu.VMEM(active.shape, active.dtype))
    scratch.append(pltpu.SemaphoreType.DMA((2 * count + 2,)))
    return call(
        functools.partial(encode_body, count, last), order, operands, [FAR] * len(operands), out,
        [whole(o.shape) for o in out],
        2 * count * rows * width * lats, 2 * count * width * (rows + lats) + 8 * rows * lats, "encode", scratch,
    )


def bring_body(order, x, out, sem):
    copy = pltpu.make_async_copy(x, out, sem)
    copy.start()
    copy.wait()


def bring(order, x):
    return call(
        bring_body, order, [x], [FAR], jax.ShapeDtypeStruct(x.shape, x.dtype),
        pl.BlockSpec(memory_space=pltpu.VMEM), 0, 4 * x.size, "bring", [pltpu.SemaphoreType.DMA],
    )


def turn_body(count, order, *refs):
    xs, (out, held, turned, in_sems, out_sems) = refs[:count], refs[count:]
    width = held.shape[2]
    loads = [pltpu.make_async_copy(xs[b], held.at[b], in_sems.at[b]) for b in range(count)]
    for load in loads:
        load.start()
    stores = []
    for b in range(count):
        loads[b].wait()
        turned[b] = held[b].T
        stores.append(pltpu.make_async_copy(turned.at[b], out.at[b], out_sems.at[b]))
        stores[-1].start()
    for store in stores:
        store.wait()


def turn(order, blocks):
    count = len(blocks)
    rows, width = blocks[0].shape
    if plain(width):
        return jnp.stack([x.T for x in blocks])
    shape = (count, width, rows)
    return call(
        functools.partial(turn_body, count), order, blocks, [FAR] * count, jax.ShapeDtypeStruct(shape, BF16), FAR,
        0, 4 * count * rows * width, "turn",
        [pltpu.VMEM((count, rows, width), BF16), pltpu.VMEM(shape, BF16),
         pltpu.SemaphoreType.DMA((count,)), pltpu.SemaphoreType.DMA((count,))],
    )


def column_specs(lats, width):
    return [pl.BlockSpec((lats, width), functools.partial(lambda m, i, order: (0, order[m]), m)) for m in range(4)]


def decode_body(order, act, w0, w1, w2, w3, *rest):
    *_, keep, send = rest
    a = act[...]
    keep[0] = jnp.dot(a, w0[...], preferred_element_type=F32)
    keep[1] = jnp.dot(a, w1[...], preferred_element_type=F32)
    send[0] = jnp.dot(a, w2[...], preferred_element_type=F32).astype(BF16)
    send[1] = jnp.dot(a, w3[...], preferred_element_type=F32).astype(BF16)


def decode(order, act, weight, width, earlier):
    rows, lats = act.shape
    if plain(width):
        terms = [jnp.dot(act, taken(weight, order[m], width, 1), preferred_element_type=F32) for m in range(4)]
        return jnp.stack(terms[:2]), jnp.stack(terms[2:]).astype(BF16)
    out = [jax.ShapeDtypeStruct((2, rows, width), F32), jax.ShapeDtypeStruct((2, rows, width), BF16)]
    return call(
        decode_body, order, [act] + [weight] * 4 + earlier,
        [whole(act.shape)] + column_specs(lats, width) + [ANYWHERE] * len(earlier), out,
        [whole((2, rows, width))] * 2, 8 * rows * width * lats, 12 * rows * width + 8 * width * lats, "decode",
    )


def backward_body(last, across, order, act, e0, e1, e2, e3, w0, w1, w2, w3, dact, squares, earlier, *rest):
    rows, width = e0.shape
    half = act.shape[1] // 2
    total = dact[...]
    square = squares[...]
    if last:
        slope, grad_keep, grad_send, dpre_keep, dpre_send, next_squares = rest
    else:
        grad_keep, grad_send, next_dact, next_squares = rest
    side = order[order.shape[0] - 1]
    mine_at = pl.ds(pl.multiple_of(side * half, half), half)
    other_at = pl.ds(pl.multiple_of((1 - side) * half, half), half)
    mine, other = act[:, mine_at], act[:, other_at]
    for m, (e, w) in enumerate(((e0, w0), (e1, w1), (e2, w2), (e3, w3))):
        block = e[...]
        total = total + lax.dot_general(block, w[...], (((1,), (1,)), ((), ())), preferred_element_type=F32)
        wide = block.astype(F32)
        square = square + jnp.sum((wide * wide).reshape(rows // 8, 8, width), axis=0)
        at, there = pl.ds(m * width, width), pl.ds(across[m] * width, width)
        grad_keep[:, at] = lax.dot_general(mine, block, (((0,), (0,)), ((), ())), preferred_element_type=F32)
        grad_send[:, there] = lax.dot_general(
            other, block, (((0,), (0,)), ((), ())), preferred_element_type=F32
        ).astype(BF16)
    if last:
        next_squares[...] = jnp.broadcast_to(jnp.sum(square, axis=(0, 1), keepdims=True), next_squares.shape)
        slope[...] = total * slope[...]
        dpre_keep[...] = slope[:, mine_at].astype(BF16)
        dpre_send[...] = slope[:, other_at].astype(BF16)
    else:
        next_dact[...] = total
        next_squares[...] = square


def backward(order, across, act, blocks, weight, dact, squares, earlier, slope):
    rows, width = blocks[0].shape
    lats = act.shape[1]
    last = slope is not None
    if plain(width):
        half, side = lats // 2, order[-1]
        mine, other = taken(act, side, half, 1), taken(act, 1 - side, half, 1)
        for e, m in zip(blocks, range(4)):
            w = taken(weight, order[m], width, 1)
            dact = dact + lax.dot_general(e, w, (((1,), (1,)), ((), ())), preferred_element_type=F32)
            squares = squares + jnp.sum(e.astype(F32) ** 2) / squares.size
        keep = jnp.concatenate([outer(mine, e) for e in blocks], axis=1)
        send = jnp.concatenate([outer(other, blocks[m]) for m in across], axis=1).astype(BF16)
        if not last:
            return keep, send, dact, squares
        dpre = (dact * slope).astype(BF16)
        squares = jnp.broadcast_to(jnp.sum(squares), (8, LANES))
        return keep, send, taken(dpre, side, half, 1), taken(dpre, 1 - side, half, 1), squares
    operands = [act] + list(blocks) + [weight] * 4 + [dact, squares, earlier]
    specs = [whole(act.shape)] + [whole((rows, width))] * 4 + column_specs(lats, width)
    specs += [whole(dact.shape), whole(squares.shape), ANYWHERE]
    if last:
        operands.append(slope)
        specs.append(whole(slope.shape))
    out = [
        jax.ShapeDtypeStruct((lats // 2, 4 * width), F32),
        jax.ShapeDtypeStruct((lats // 2, 4 * width), BF16),
    ]
    if last:
        out += [jax.ShapeDtypeStruct((rows, lats // 2), BF16)] * 2
    else:
        out.append(jax.ShapeDtypeStruct((rows, lats), F32))
    out.append(jax.ShapeDtypeStruct((8, 128) if last else squares.shape, F32))
    return call(
        functools.partial(backward_body, last, across), order, operands, specs, out, [whole(o.shape) for o in out],
        16 * rows * width * lats, 8 * rows * width + 20 * width * lats + 8 * rows * lats, "backward",
    )


def decoder_gradient_body(slots, width, scale, order, *refs):
    keeps, gots, (square, square_got, out, mean) = refs[:slots], refs[slots:2 * slots], refs[2 * slots:]
    mean[...] = (square[0:1, 0:1] + square_got[0:1, 0:1]) * scale
    for s in range(slots):
        for m in range(4):
            at = pl.ds(m * width, width)
            there = pl.ds(pl.multiple_of(order[4 * s + m] * width, width), width)
            out[:, there] = keeps[s][:, at] + gots[s][:, at].astype(F32)


def decoder_gradient(order, keeps, gots, width, squares, count):
    slots = len(keeps)
    half = keeps[0].shape[0]
    operands = keeps + gots + list(squares)
    size = half * 4 * slots * width
    if plain(width):
        out = jnp.zeros((half, 4 * slots * width), F32)
        for s in range(slots):
            part = keeps[s] + gots[s].astype(F32)
            for m in range(4):
                block = part[:, m * width:(m + 1) * width]
                out = lax.dynamic_update_slice_in_dim(out, block, order[4 * s + m] * width, 1)
        return out, (squares[0] + squares[1])[:1, :1] / count
    return call(
        functools.partial(decoder_gradient_body, slots, width, 1.0 / count), order, operands,
        [whole(o.shape) for o in operands],
        [jax.ShapeDtypeStruct((half, 4 * slots * width), F32), jax.ShapeDtypeStruct((1, 1), F32)],
        [whole((half, 4 * slots * width)), whole((1, 1))], size, 10 * size,
        "decoder_gradient",
    )


def encoder_gradient_body(slots, width, across, order, mine, theirs, dpre, got, out):
    d, g = dpre[...], got[...]
    for s in range(slots):
        for m in range(4):
            here = jnp.dot(mine[4 * s + m], d, preferred_element_type=F32)
            here += jnp.dot(theirs[4 * s + across[m]], g, preferred_element_type=F32)
            out[pl.ds(pl.multiple_of(order[4 * s + m] * width, width), width), :] = here


def encoder_gradient(order, across, mine, theirs, dpre, got):
    count, width, rows = mine.shape
    slots, half = count // 4, dpre.shape[1]
    operands = [mine, theirs, dpre, got]
    shape = (count * width, half)
    if plain(width):
        out = jnp.zeros(shape, F32)
        for b in range(count):
            block = jnp.dot(mine[b], dpre, preferred_element_type=F32)
            block += jnp.dot(theirs[b - b % 4 + across[b % 4]], got, preferred_element_type=F32)
            out = lax.dynamic_update_slice_in_dim(out, block, order[b] * width, 0)
        return out
    return call(
        functools.partial(encoder_gradient_body, slots, width, across), order, operands,
        [whole(o.shape) for o in operands], jax.ShapeDtypeStruct(shape, F32), whole(shape),
        4 * shape[0] * rows * half, 4 * shape[0] * (rows + half), "encoder_gradient",
    )


def local(lat, dp, inputs, dec_bias, enc_weight, enc_bias, dec_weight, other_recon, active_blocks):
    grid = Grid(lat, dp)
    rows, width = inputs.shape
    lats = enc_weight.shape[1]
    half = lats // 2
    slots = grid.slots
    centered = grid.gather((inputs.astype(F32) - dec_bias.astype(F32)[None, :]).astype(BF16))
    centered = [block for slot in centered for block in slot]
    near = dec_weight if plain(width) else bring(grid.every, dec_weight)
    (pre_act,) = encode(grid.every[:-4], centered[:-4], enc_weight, enc_bias[None, :], None)
    act, slope = encode(grid.every[-4:], centered[-4:], enc_weight, pre_act, active_blocks.T)
    turned = turn(grid.every, centered)
    theirs = grid.swap_core(turned)

    def part(s, earlier):
        earlier = [] if earlier is None else [earlier]
        if s == slots // 2 - 1:
            earlier.append(turned)
        return decode(grid.order[s], act, near, width, earlier)

    recon = grid.scatter_sum(part)
    bias, x = dec_bias.astype(F32), inputs.astype(F32)
    error_local = recon + (other_recon + bias[None, :]) - x
    state = [jnp.zeros((rows, lats), F32), jnp.zeros((8, width), F32)]
    keeps, gots = [], []

    for s, blocks in enumerate(grid.gather(error_local.astype(BF16))):
        order = grid.order[s]
        keep, send, *state[:] = backward(
            order, grid.across, act, blocks, near, *state, theirs if s == 0 else order, slope if s == slots - 1 else None
        )
        keeps.append(keep)
        gots.append(grid.swap_core(send))

    mine, other, squares = state

    square, step = squares, 1
    while step < dp:
        square_got = lax.ppermute(square, "dp", [(d, d ^ step) for d in range(dp)])
        step *= 2
        if step < dp:
            square = square + square_got
    got = grid.swap_core(other)
    grad_dec, mean = decoder_gradient(
        grid.every, keeps, gots, width, (square, square_got), rows * dp * width * lat
    )
    mse_loss = mean.reshape(())
    grad_enc = encoder_gradient(grid.every, grid.across, turned, theirs, mine, got)

    return (error_local, mse_loss, grid.spread(grad_dec, 0), grid.spread(grad_enc, 1))


def solution(mesh):
    placed = (
        P("dp", "lat"),
        P("lat"),
        P(None, "lat"),
        P("lat"),
        P("lat", None),
        P("dp", "lat"),
        P("dp", "lat"),
    )
    lat, dp = mesh.shape["lat"], mesh.shape["dp"]
    return jax.shard_map(
        functools.partial(local, lat, dp),
        mesh=mesh,
        in_specs=placed,
        out_specs=(P("dp", "lat"), P(), P(("lat", "dp"), None), P(None, ("lat", "dp"))),
        check_vma=False,
    )
```

```python
import functools

import jax
import jax.numpy as jnp
from jax import lax
from jax.experimental import pallas as pl
from jax.experimental.pallas import tpu as pltpu
from jax.sharding import PartitionSpec as P


F32, BF16 = jnp.float32, jnp.bfloat16
VMEM_BYTES = 24 * 1024 * 1024
LANES = 128


class Grid:
    def __init__(self, lat, dp):
        self.lat, self.dp, self.slots = lat, dp, lat // 4
        self.me = lax.axis_index("lat")
        self.rank = lax.axis_index("dp")
        first = jnp.where(self.rank % 2 == 0, 1, 2)
        members = jnp.stack([jnp.zeros_like(first), first, 3 - first, jnp.full_like(first, 3)])
        self.across = (0, 2, 1, 3) if dp == 2 else (0, 1, 2, 3)
        side = self.rank // (dp // 2)
        orders = [self.me ^ (4 * s + members) for s in range(self.slots)]
        self.order = [jnp.append(o, side).astype(jnp.int32) for o in orders]
        self.every = jnp.concatenate(orders).astype(jnp.int32)

    def swap(self, x, even, odd):
        pairs = []
        for i in range(self.lat):
            for d in range(self.dp):
                pairs.append((i * self.dp + d, (i ^ (even if d % 2 == 0 else odd)) * self.dp + d))
        return lax.ppermute(x, ("lat", "dp"), pairs)

    def swap_first(self, x):
        return self.swap(x, 1, 2)

    def swap_second(self, x):
        return self.swap(x, 2, 1)

    def swap_plane(self, x, bit):
        return self.swap(x, 4 * bit, 4 * bit)

    def swap_core(self, x):
        pairs = []
        for i in range(self.lat):
            for d in range(self.dp):
                pairs.append((i * self.dp + d, i * self.dp + (d ^ self.dp // 2)))
        return lax.ppermute(x, ("lat", "dp"), pairs)

    def spread(self, x, axis):
        h = self.dp // 4
        while h >= 1:
            bit = self.rank // h % 2
            size = x.shape[axis] // 2
            mine = lax.dynamic_slice_in_dim(x, bit * size, size, axis)
            other = lax.dynamic_slice_in_dim(x, (1 - bit) * size, size, axis)
            x = mine + lax.ppermute(other, "dp", [(d, d ^ h) for d in range(self.dp)])
            h //= 2
        return x

    def gather(self, own):
        column = [own]
        for s in range(1, self.slots):
            column.append(self.swap_plane(column[s & (s - 1)], s & -s))
        seconds = []
        for s, block in enumerate(column):
            seconds.append(self.swap_plane(seconds[-1], 1) if s % 2 else self.swap_first(block))
        return [(b, a, self.swap_second(b), self.swap_second(a)) for b, a in zip(column, seconds)]

    def scatter_sum(self, part):
        column = [None] * self.slots
        earlier = {}
        last = self.slots - 1
        moved = None
        for s in reversed(range(self.slots)):
            keep, send = part(s, earlier.get(s))
            there = self.swap_second(send)
            pair = keep + there.astype(F32)
            if s == last > 1:
                other = self.swap_plane(pair[1].astype(BF16), 1)
                moved = (self.swap_plane(pair[0].astype(BF16), 1), other)
                earlier = {s - 2: there, s - 3: other}
                continue
            mine, other = pair[0], pair[1]
            if s == last - 1:
                mine, other = mine + moved[0].astype(F32), other + moved[1].astype(F32)
            got = self.swap_first(other.astype(BF16))
            column[s] = mine + got.astype(F32)
        for s in reversed(range(1, self.slots)):
            if column[s] is not None:
                t = s & (s - 1)
                send = column[s].astype(BF16)
                column[t] = column[t] + self.swap_plane(send, s & -s).astype(F32)
        return column[0]


def plain(width):
    return width % LANES != 0


def taken(x, index, width, axis):
    return lax.dynamic_slice_in_dim(x, index * width, width, axis)


def gate_of(active, lats):
    blocks, rows = active.shape
    turned = active.astype(F32).T
    return jnp.concatenate(
        [jnp.broadcast_to(turned[:, b:b + 1], (rows, lats // blocks)) for b in range(blocks)], axis=1
    )


def activate(total, active):
    positive = jnp.maximum(total, 0.0)
    gated = positive * gate_of(active, total.shape[1])
    return (positive * gated).astype(BF16), 2.0 * gated


def outer(a, b):
    return lax.dot_general(a, b, (((0,), (0,)), ((), ())), preferred_element_type=F32)


def call(body, order, operands, in_specs, out_shape, out_specs, flops, moved, name, scratch=()):
    return pl.pallas_call(
        body,
        grid_spec=pltpu.PrefetchScalarGridSpec(
            num_scalar_prefetch=1, grid=(1,), in_specs=in_specs, out_specs=out_specs, scratch_shapes=scratch
        ),
        out_shape=out_shape,
        compiler_params=pltpu.CompilerParams(vmem_limit_bytes=VMEM_BYTES),
        cost_estimate=pl.CostEstimate(flops=flops, bytes_accessed=moved, transcendentals=0),
        name=name,
    )(order, *operands)


ANYWHERE = pl.BlockSpec(memory_space=pl.ANY)
FAR = pl.BlockSpec(memory_space=pltpu.HBM)


def whole(shape):
    return pl.BlockSpec(shape, lambda i, order: (0,) * len(shape))


def encode_body(count, last, order, *refs):
    xs, (weight, start, *refs) = refs[:count], refs[count:]
    width = xs[0].shape[1]
    if last:
        active, act, slope, held, rows_of, begun, gates, sems = refs
        pairs = [(active, gates)]
    else:
        total_out, held, rows_of, begun, sems = refs
        pairs = []
    pairs.append((start, begun))
    for b in range(count):
        at = pl.ds(pl.multiple_of(order[b] * width, width), width)
        here = pl.ds(b * width, width)
        pairs += [(xs[b], held.at[:, here]), (weight.at[at], rows_of.at[here])]
    loads = [pltpu.make_async_copy(a, b, sems.at[n]) for n, (a, b) in enumerate(pairs)]
    for load in loads:
        load.start()
    for load in loads[:-2 * count]:
        load.wait()
    total = begun[...]
    for b in range(0, count, 4):
        for load in loads[2 * (b - count):][:8]:
            load.wait()
        here = pl.ds(b * width, 4 * width)
        total = total + jnp.dot(held[:, here], rows_of[here, :], preferred_element_type=F32)
    if last:
        act[...], slope[...] = activate(total, gates[...])
    else:
        total_out[...] = total


def encode(order, blocks, weight, start, active):
    count = len(blocks)
    rows, width = blocks[0].shape
    lats = weight.shape[1]
    last = active is not None
    if plain(width):
        total = start
        for b in range(count):
            total = total + jnp.dot(blocks[b], taken(weight, order[b], width, 0), preferred_element_type=F32)
        return activate(total, active) if last else [total]
    out = [jax.ShapeDtypeStruct((rows, lats), F32)]
    operands = blocks + [weight, start]
    scratch = [pltpu.VMEM((rows, count * width), BF16), pltpu.VMEM((count * width, lats), BF16)]
    scratch.append(pltpu.VMEM(start.shape, F32))
    if last:
        out = [jax.ShapeDtypeStruct((rows, lats), BF16)] + out
        operands.append(active)
        scratch.append(pltpu.VMEM(active.shape, active.dtype))
    scratch.append(pltpu.SemaphoreType.DMA((2 * count + 2,)))
    return call(
        functools.partial(encode_body, count, last), order, operands, [FAR] * len(operands), out,
        [whole(o.shape) for o in out],
        2 * count * rows * width * lats, 2 * count * width * (rows + lats) + 8 * rows * lats, "encode", scratch,
    )


def bring_body(order, x, out, sem):
    copy = pltpu.make_async_copy(x, out, sem)
    copy.start()
    copy.wait()


def bring(order, x):
    return call(
        bring_body, order, [x], [FAR], jax.ShapeDtypeStruct(x.shape, x.dtype),
        pl.BlockSpec(memory_space=pltpu.VMEM), 0, 4 * x.size, "bring", [pltpu.SemaphoreType.DMA],
    )


def turn_body(count, order, *refs):
    xs, (out, held, turned, in_sems, out_sems) = refs[:count], refs[count:]
    width = held.shape[2]
    loads = [pltpu.make_async_copy(xs[b], held.at[b], in_sems.at[b]) for b in range(count)]
    for load in loads:
        load.start()
    stores = []
    for b in range(count):
        loads[b].wait()
        turned[b] = held[b].T
        stores.append(pltpu.make_async_copy(turned.at[b], out.at[b], out_sems.at[b]))
        stores[-1].start()
    for store in stores:
        store.wait()


def turn(order, blocks):
    count = len(blocks)
    rows, width = blocks[0].shape
    if plain(width):
        return jnp.stack([x.T for x in blocks])
    shape = (count, width, rows)
    return call(
        functools.partial(turn_body, count), order, blocks, [FAR] * count, jax.ShapeDtypeStruct(shape, BF16), FAR,
        0, 4 * count * rows * width, "turn",
        [pltpu.VMEM((count, rows, width), BF16), pltpu.VMEM(shape, BF16),
         pltpu.SemaphoreType.DMA((count,)), pltpu.SemaphoreType.DMA((count,))],
    )


def column_specs(lats, width):
    return [pl.BlockSpec((lats, width), functools.partial(lambda m, i, order: (0, order[m]), m)) for m in range(4)]


def decode_body(order, act, w0, w1, w2, w3, *rest):
    *_, keep, send = rest
    a = act[...]
    keep[0] = jnp.dot(a, w0[...], preferred_element_type=F32)
    keep[1] = jnp.dot(a, w1[...], preferred_element_type=F32)
    send[0] = jnp.dot(a, w2[...], preferred_element_type=F32).astype(BF16)
    send[1] = jnp.dot(a, w3[...], preferred_element_type=F32).astype(BF16)


def decode(order, act, weight, width, earlier):
    rows, lats = act.shape
    if plain(width):
        terms = [jnp.dot(act, taken(weight, order[m], width, 1), preferred_element_type=F32) for m in range(4)]
        return jnp.stack(terms[:2]), jnp.stack(terms[2:]).astype(BF16)
    out = [jax.ShapeDtypeStruct((2, rows, width), F32), jax.ShapeDtypeStruct((2, rows, width), BF16)]
    return call(
        decode_body, order, [act] + [weight] * 4 + earlier,
        [whole(act.shape)] + column_specs(lats, width) + [ANYWHERE] * len(earlier), out,
        [whole((2, rows, width))] * 2, 8 * rows * width * lats, 12 * rows * width + 8 * width * lats, "decode",
    )


def backward_body(last, across, order, act, e0, e1, e2, e3, w0, w1, w2, w3, dact, squares, earlier, *rest):
    rows, width = e0.shape
    half = act.shape[1] // 2
    total = dact[...]
    square = squares[...]
    if last:
        slope, grad_keep, grad_send, dpre_keep, dpre_send, next_squares = rest
    else:
        grad_keep, grad_send, next_dact, next_squares = rest
    side = order[order.shape[0] - 1]
    mine_at = pl.ds(pl.multiple_of(side * half, half), half)
    other_at = pl.ds(pl.multiple_of((1 - side) * half, half), half)
    mine, other = act[:, mine_at], act[:, other_at]
    for m, (e, w) in enumerate(((e0, w0), (e1, w1), (e2, w2), (e3, w3))):
        block = e[...]
        total = total + lax.dot_general(block, w[...], (((1,), (1,)), ((), ())), preferred_element_type=F32)
        wide = block.astype(F32)
        square = square + jnp.sum((wide * wide).reshape(rows // 8, 8, width), axis=0)
        at, there = pl.ds(m * width, width), pl.ds(across[m] * width, width)
        grad_keep[:, at] = lax.dot_general(mine, block, (((0,), (0,)), ((), ())), preferred_element_type=F32)
        grad_send[:, there] = lax.dot_general(
            other, block, (((0,), (0,)), ((), ())), preferred_element_type=F32
        ).astype(BF16)
    if last:
        next_squares[...] = jnp.broadcast_to(jnp.sum(square, axis=(0, 1), keepdims=True), next_squares.shape)
        slope[...] = total * slope[...]
        dpre_keep[...] = slope[:, mine_at].astype(BF16)
        dpre_send[...] = slope[:, other_at].astype(BF16)
    else:
        next_dact[...] = total
        next_squares[...] = square


def backward(order, across, act, blocks, weight, dact, squares, earlier, slope):
    rows, width = blocks[0].shape
    lats = act.shape[1]
    last = slope is not None
    if plain(width):
        half, side = lats // 2, order[-1]
        mine, other = taken(act, side, half, 1), taken(act, 1 - side, half, 1)
        for e, m in zip(blocks, range(4)):
            w = taken(weight, order[m], width, 1)
            dact = dact + lax.dot_general(e, w, (((1,), (1,)), ((), ())), preferred_element_type=F32)
            squares = squares + jnp.sum(e.astype(F32) ** 2) / squares.size
        keep = jnp.concatenate([outer(mine, e) for e in blocks], axis=1)
        send = jnp.concatenate([outer(other, blocks[m]) for m in across], axis=1).astype(BF16)
        if not last:
            return keep, send, dact, squares
        dpre = (dact * slope).astype(BF16)
        squares = jnp.broadcast_to(jnp.sum(squares), (8, LANES))
        return keep, send, taken(dpre, side, half, 1), taken(dpre, 1 - side, half, 1), squares
    operands = [act] + list(blocks) + [weight] * 4 + [dact, squares, earlier]
    specs = [whole(act.shape)] + [whole((rows, width))] * 4 + column_specs(lats, width)
    specs += [whole(dact.shape), whole(squares.shape), ANYWHERE]
    if last:
        operands.append(slope)
        specs.append(whole(slope.shape))
    out = [
        jax.ShapeDtypeStruct((lats // 2, 4 * width), F32),
        jax.ShapeDtypeStruct((lats // 2, 4 * width), BF16),
    ]
    if last:
        out += [jax.ShapeDtypeStruct((rows, lats // 2), BF16)] * 2
    else:
        out.append(jax.ShapeDtypeStruct((rows, lats), F32))
    out.append(jax.ShapeDtypeStruct((8, 128) if last else squares.shape, F32))
    return call(
        functools.partial(backward_body, last, across), order, operands, specs, out, [whole(o.shape) for o in out],
        16 * rows * width * lats, 8 * rows * width + 20 * width * lats + 8 * rows * lats, "backward",
    )


def decoder_gradient_body(slots, width, scale, order, *refs):
    keeps, gots, (square, square_got, out, mean) = refs[:slots], refs[slots:2 * slots], refs[2 * slots:]
    mean[...] = (square[0:1, 0:1] + square_got[0:1, 0:1]) * scale
    for s in range(slots):
        for m in range(4):
            at = pl.ds(m * width, width)
            there = pl.ds(pl.multiple_of(order[4 * s + m] * width, width), width)
            out[:, there] = keeps[s][:, at] + gots[s][:, at].astype(F32)


def decoder_gradient(order, keeps, gots, width, squares, count):
    slots = len(keeps)
    half = keeps[0].shape[0]
    operands = keeps + gots + list(squares)
    size = half * 4 * slots * width
    if plain(width):
        out = jnp.zeros((half, 4 * slots * width), F32)
        for s in range(slots):
            part = keeps[s] + gots[s].astype(F32)
            for m in range(4):
                block = part[:, m * width:(m + 1) * width]
                out = lax.dynamic_update_slice_in_dim(out, block, order[4 * s + m] * width, 1)
        return out, (squares[0] + squares[1])[:1, :1] / count
    return call(
        functools.partial(decoder_gradient_body, slots, width, 1.0 / count), order, operands,
        [whole(o.shape) for o in operands],
        [jax.ShapeDtypeStruct((half, 4 * slots * width), F32), jax.ShapeDtypeStruct((1, 1), F32)],
        [whole((half, 4 * slots * width)), whole((1, 1))], size, 10 * size,
        "decoder_gradient",
    )


def encoder_gradient_body(slots, width, across, order, mine, theirs, dpre, got, out):
    d, g = dpre[...], got[...]
    for s in range(slots):
        for m in range(4):
            here = jnp.dot(mine[4 * s + m], d, preferred_element_type=F32)
            here += jnp.dot(theirs[4 * s + across[m]], g, preferred_element_type=F32)
            out[pl.ds(pl.multiple_of(order[4 * s + m] * width, width), width), :] = here


def encoder_gradient(order, across, mine, theirs, dpre, got):
    count, width, rows = mine.shape
    slots, half = count // 4, dpre.shape[1]
    operands = [mine, theirs, dpre, got]
    shape = (count * width, half)
    if plain(width):
        out = jnp.zeros(shape, F32)
        for b in range(count):
            block = jnp.dot(mine[b], dpre, preferred_element_type=F32)
            block += jnp.dot(theirs[b - b % 4 + across[b % 4]], got, preferred_element_type=F32)
            out = lax.dynamic_update_slice_in_dim(out, block, order[b] * width, 0)
        return out
    return call(
        functools.partial(encoder_gradient_body, slots, width, across), order, operands,
        [whole(o.shape) for o in operands], jax.ShapeDtypeStruct(shape, F32), whole(shape),
        4 * shape[0] * rows * half, 4 * shape[0] * (rows + half), "encoder_gradient",
    )


def local(lat, dp, inputs, dec_bias, enc_weight, enc_bias, dec_weight, other_recon, active_blocks):
    grid = Grid(lat, dp)
    rows, width = inputs.shape
    lats = enc_weight.shape[1]
    half = lats // 2
    slots = grid.slots
    centered = grid.gather((inputs.astype(F32) - dec_bias.astype(F32)[None, :]).astype(BF16))
    centered = [block for slot in centered for block in slot]
    near = dec_weight if plain(width) else bring(grid.every, dec_weight)
    (pre_act,) = encode(grid.every[:-4], centered[:-4], enc_weight, enc_bias[None, :], None)
    act, slope = encode(grid.every[-4:], centered[-4:], enc_weight, pre_act, active_blocks.T)
    turned = turn(grid.every, centered)
    theirs = grid.swap_core(turned)

    def part(s, earlier):
        earlier = [] if earlier is None else [earlier]
        if s == slots // 2 - 1:
            earlier.append(turned)
        return decode(grid.order[s], act, near, width, earlier)

    recon = grid.scatter_sum(part)
    bias, x = dec_bias.astype(F32), inputs.astype(F32)
    error_local = recon + (other_recon + bias[None, :]) - x
    state = [jnp.zeros((rows, lats), F32), jnp.zeros((8, width), F32)]
    keeps, gots = [], []

    for s, blocks in enumerate(grid.gather(error_local.astype(BF16))):
        order = grid.order[s]
        keep, send, *state[:] = backward(
            order, grid.across, act, blocks, near, *state, theirs if s == 0 else order, slope if s == slots - 1 else None
        )
        keeps.append(keep)
        gots.append(grid.swap_core(send))

    mine, other, squares = state

    square, step = squares, 1
    while step < dp:
        square_got = lax.ppermute(square, "dp", [(d, d ^ step) for d in range(dp)])
        step *= 2
        if step < dp:
            square = square + square_got
    got = grid.swap_core(other)
    grad_dec, mean = decoder_gradient(
        grid.every, keeps, gots, width, (square, square_got), rows * dp * width * lat
    )
    mse_loss = mean.reshape(())
    grad_enc = encoder_gradient(grid.every, grid.across, turned, theirs, mine, got)

    return (error_local, mse_loss, grid.spread(grad_dec, 0), grid.spread(grad_enc, 1))


def solution(mesh):
    placed = (
        P("dp", "lat"),
        P("lat"),
        P(None, "lat"),
        P("lat"),
        P("lat", None),
        P("dp", "lat"),
        P("dp", "lat"),
    )
    lat, dp = mesh.shape["lat"], mesh.shape["dp"]
    return jax.shard_map(
        functools.partial(local, lat, dp),
        mesh=mesh,
        in_specs=placed,
        out_specs=(P("dp", "lat"), P(), P(("lat", "dp"), None), P(None, ("lat", "dp"))),
        check_vma=False,
    )
```
